512 devices in a mesh: queue: 32 (over y_hi, z), mp: 16 (over x, y_lo, core).
Axes of the slice: x: 4, y: 4 (y_hi: 2, y_lo: 2; y = y_hi * 2 + y_lo), z: 16, core: 2. Of those that a mesh axis runs over, the one named last changes fastest.
Arguments:
- latents: bfloat16 [32, 768, 1152], P('queue', 'mp'), may hold values from -6 to 6
- fresh_noise: bfloat16 [768, 1152], P('mp'), may hold values from -6 to 6
- levels: int32 [32], P('queue'), may hold values from 0 to 31, each once
- modulation: float32 [32, 6, 1152], replicated, may hold values from -1 to 11, as said below
- head_map: int32 [16], P('mp'), may hold values from 0 to 15, each once
- window: int32 [16], replicated, may hold values from 1 to 2, as said below
- qkv_weight: bfloat16 [1152, 3456], P(None, 'mp'), may hold values from -0.1875 to 0.1875
- out_weight: bfloat16 [1152, 1152], P('mp'), may hold values from -0.1875 to 0.1875
- fc1_weight: bfloat16 [1152, 4608], P(None, 'mp'), may hold values from -0.1875 to 0.1875
- fc2_weight: bfloat16 [4608, 1152], P('mp'), may hold values from -0.09375 to 0.09375
Outputs:
- queue_next: bfloat16 [32, 768, 1152], P('queue', 'mp')
The draws below stay inside these ranges and needn't reach their ends.
Inputs may be any that keep to these rules, and one draw needn't show every extreme that they name: `window`: every head's half-width lies in 1..2 and some head has exactly 2. `modulation`: shift entries in -1..1, gates in 0.3..1.5, scale entries in -0.5..11.
All inputs are finite; a program needn't handle non-finite values.
Results may differ from the reference program's by a relative error of at most 0.025.
Values may be sent and summed in bfloat16 or wider, within the bound.
No kernel may reach another device: no remote copies, remote signals or barrier semaphores. Data moves between devices by JAX's collectives and lax.ppermute only.
A program may use at most 64 MiB of HBM per device.

```python
import jax
import jax.numpy as jnp
from jax import lax

D = 1152
HEADS = 16
HD = 72
FF = 4608
WMAX = 2
TOKENS_F = 768
FRAMES = 32
LEVELS = 32
N_MP = 16


def draw_modulation(key, part):
    key = jax.random.fold_in(key, 11)
    keys = jax.random.split(key, 6)
    shape = (LEVELS, D)
    shift_one = jax.random.uniform(keys[0], shape, jnp.float32, -1.0, 1.0)
    scale_one = jax.random.uniform(keys[1], shape, jnp.float32, -0.5, 1.0)
    gate_one = jax.random.uniform(keys[2], shape, jnp.float32, 0.3, 1.5)
    shift_two = jax.random.uniform(keys[3], shape, jnp.float32, -1.0, 1.0)
    scale_two = jax.random.uniform(keys[4], shape, jnp.float32, -0.5, 1.0)
    gate_two = jax.random.uniform(keys[5], shape, jnp.float32, 0.3, 1.5)
    return jnp.stack([shift_one, scale_one, gate_one, shift_two, scale_two, gate_two], axis=1)


def draw_window(key, part):
    key = jax.random.fold_in(key, 23)
    first, second = jax.random.split(key)
    widths = jax.random.randint(first, (HEADS,), 1, WMAX + 1)
    picked = jax.random.randint(second, (), 0, HEADS)
    return jnp.where(jnp.arange(HEADS) == picked, WMAX, widths).astype(jnp.int32)


def level_of(rng, shape, pieces, low, high):
    def one(position, blocks):
        steps = jax.random.uniform(jax.random.fold_in(jax.random.fold_in(rng, 6), position), (blocks,), jnp.float32, low / len(pieces), high / len(pieces))
        return jnp.repeat(jnp.exp(steps), shape[position] // blocks).reshape((-1,) + (1,) * (len(shape) - position - 1))

    loudness = one(*pieces[0])
    for cut in pieces[1:]:
        loudness = loudness * one(*cut)
    return loudness


def noise(own_key, extent, deviation, most, shards=(), held_as=jnp.bfloat16):
    factor_of = level_of(own_key, extent, shards, -0.22, 0.18) if shards else 1.0
    result = jax.random.normal(own_key, extent, jnp.float32) * deviation * factor_of
    return jnp.minimum(jnp.maximum(result, -most), most).astype(held_as)


def setup_inputs(seed: int = 0) -> dict:
    arg_keys = jax.random.split(jax.random.key(seed), 11)
    return {
        "latents": noise(arg_keys[0], (FRAMES, TOKENS_F, D), 1.0, 6.0, ((0, 32), (1, 16))),
        "fresh_noise": noise(arg_keys[1], (TOKENS_F, D), 1.0, 6.0, ((0, 16),)),
        "levels": jax.random.permutation(arg_keys[2], FRAMES).astype(jnp.int32),
        "modulation": draw_modulation(jax.random.fold_in(arg_keys[10], 71), 0),
        "head_map": jax.random.permutation(arg_keys[4], HEADS).astype(jnp.int32),
        "window": draw_window(jax.random.fold_in(arg_keys[10], 71), 0),
        "qkv_weight": noise(arg_keys[6], (D, 3 * HEADS * HD), D ** -0.5, 0.1875, ((1, 16),)),
        "out_weight": noise(arg_keys[7], (HEADS * HD, D), (HEADS * HD) ** -0.5, 0.1875, ((0, 16),)),
        "fc1_weight": noise(arg_keys[8], (D, FF), D ** -0.5, 0.1875, ((1, 16),)),
        "fc2_weight": noise(arg_keys[9], (FF, D), FF ** -0.5, 0.09375, ((0, 16),)),
    }


def modulate(values, shift, scale):
    floats = values.astype(jnp.float32)
    center = lax.optimization_barrier(jnp.mean(floats, axis=-1, keepdims=True))
    spread = lax.optimization_barrier(jnp.mean((floats - center) ** 2, axis=-1, keepdims=True))
    return ((floats - center) * lax.rsqrt(spread + 1e-06) * (1.0 + scale) + shift).astype(jnp.bfloat16)

def neighbor(array, offset):
    if offset == 0:
        return array
    filler = jnp.zeros((abs(offset),) + array.shape[1:], array.dtype)
    if offset > 0:
        return jnp.concatenate([array[offset:], filler], axis=0)
    return jnp.concatenate([filler, array[:offset]], axis=0)

def reference(latents, fresh_noise, levels, modulation, head_map, window, qkv_weight, out_weight, fc1_weight, fc2_weight):
    frame_count = latents.shape[0]
    tokens_frame = latents.shape[1]
    width = latents.shape[2]
    mod = modulation[levels]
    normed = modulate(latents, mod[:, None, 0], mod[:, None, 1])
    qkv = jnp.dot(normed.reshape(-1, width), qkv_weight, preferred_element_type=jnp.float32).astype(jnp.bfloat16)
    qkv = qkv.reshape(frame_count, tokens_frame, HEADS, 3, HD).astype(jnp.float32)
    query = qkv[:, :, :, 0]
    keys = qkv[:, :, :, 1]
    values = qkv[:, :, :, 2]
    half_width = window[head_map]
    frame_index = jnp.arange(frame_count)
    scores = []
    valids = []
    value_list = []
    for offset in range(-WMAX, WMAX + 1):
        keys_here = neighbor(keys, offset)
        scores.append(lax.optimization_barrier(jnp.sum(query * keys_here, axis=-1)) / jnp.sqrt(jnp.float32(HD)))
        target = frame_index + offset
        inside = (target >= 0) & (target < frame_count)
        valids.append(inside[:, None, None] & (abs(offset) <= half_width)[None, None, :])
        value_list.append(neighbor(values, offset))
    scores = jnp.stack(scores)
    valids = jnp.stack(valids)
    masked = jnp.where(valids, scores, jnp.float32(-1e+30))
    top = lax.optimization_barrier(jnp.max(masked, axis=0, keepdims=True))
    expo = jnp.where(valids, jnp.exp(masked - top), jnp.float32(0.0))
    probs = expo / lax.optimization_barrier(jnp.sum(expo, axis=0, keepdims=True))
    attended = lax.optimization_barrier(jnp.sum(probs[..., None] * jnp.stack(value_list), axis=0)).astype(jnp.bfloat16)
    attended = attended.reshape(frame_count, tokens_frame, N_MP, HEADS * HD // N_MP)
    out_groups = out_weight.reshape(N_MP, HEADS * HD // N_MP, width).astype(jnp.float32)
    fc1_float = fc1_weight
    fc2_groups = fc2_weight.reshape(N_MP, FF // N_MP, width).astype(jnp.float32)

    def one_frame(inputs):
        frame_attended, frame_latents, frame_mod = inputs
        parts = jnp.einsum('tgc,gcd->gtd', frame_attended.astype(jnp.float32), out_groups)
        attn = lax.optimization_barrier(jnp.sum(parts.astype(jnp.bfloat16).astype(jnp.float32), axis=0))
        resid = (frame_latents.astype(jnp.float32) + frame_mod[2] * attn).astype(jnp.bfloat16)
        normed_two = modulate(resid, frame_mod[3], frame_mod[4])
        hidden = jax.nn.gelu(jnp.dot(normed_two, fc1_float, preferred_element_type=jnp.float32), approximate=True).astype(jnp.bfloat16)
        hidden = hidden.reshape(tokens_frame, N_MP, FF // N_MP)
        parts_two = jnp.einsum('tgc,gcd->gtd', hidden.astype(jnp.float32), fc2_groups)
        mlp = lax.optimization_barrier(jnp.sum(parts_two.astype(jnp.bfloat16).astype(jnp.float32), axis=0))
        return (resid.astype(jnp.float32) + frame_mod[5] * mlp).astype(jnp.bfloat16)
    block_out = lax.map(one_frame, (attended, latents, mod))
    return jnp.concatenate([fresh_noise[None], block_out[:-1]], axis=0)
```

```python
import jax
import jax.numpy as jnp
from jax import lax
from jax.experimental import pallas as pl
from jax.experimental.pallas import tpu as pltpu
from jax.sharding import Mesh
from jax.sharding import PartitionSpec as P

WMAX = 2
VMEM_LIMIT = 48 * 1024 * 1024
BF16, F32 = jnp.bfloat16, jnp.float32
SLOTS = ("yhi", "z")
SWAP = [(0, 1), (1, 0)]
FAR_Y = [(0, 3), (3, 0), (1, 2), (2, 1)]
PARAMS = pltpu.CompilerParams(vmem_limit_bytes=VMEM_LIMIT)


def normalise(floats, shift, scale):
    center = jnp.mean(floats, axis=-1, keepdims=True)
    spread = jnp.mean((floats - center) ** 2, axis=-1, keepdims=True)
    return ((floats - center) * lax.rsqrt(spread + 1e-06) * (1.0 + scale) + shift).astype(BF16)


def halves(value):
    high = value.astype(BF16)
    return high, (value - high.astype(F32)).astype(BF16)


def dot2(value, indicator):
    high, low = halves(value)
    return jnp.dot(high, indicator, preferred_element_type=F32) + jnp.dot(
        low, indicator, preferred_element_type=F32
    )


def qkv_kernel(head, width, tok_ref, mod_ref, w0, w1, w2, w3, q_ref, kv_ref, half_ref):
    normed = normalise(tok_ref[...].astype(F32), mod_ref[0:1, :], mod_ref[1:2, :])
    queries, keys, values = [], [], []
    lane = lax.broadcasted_iota(jnp.int32, half_ref.shape, 1)
    half = jnp.zeros(half_ref.shape, F32)
    for slot, weight in enumerate((w0, w1, w2, w3)):
        part = jnp.dot(normed, weight[0:width, :], preferred_element_type=F32)
        queries.append(part[:, :head])
        keys.append(part[:, head : 2 * head])
        values.append(part[:, 2 * head :])
        half = jnp.where(lane == slot, weight[width : width + 16, 0:128].astype(F32), half)
    q_ref[...] = jnp.concatenate(queries, axis=1).astype(BF16)
    kv_ref[...] = jnp.concatenate(keys + values, axis=1).astype(BF16)
    half_ref[...] = half


def attention_kernel(head, frames, frame_ref, half_ref, q_ref, k0, k1, k2, k3, k4, out_ref):
    rows, cols = q_ref.shape
    col = lax.broadcasted_iota(jnp.int32, (cols, 128), 0)
    lane = lax.broadcasted_iota(jnp.int32, (cols, 128), 1)
    gather = ((col >= lane * head) & (col < (lane + 1) * head)).astype(F32).astype(BF16)
    col = lax.broadcasted_iota(jnp.int32, (128, cols), 1)
    lane = lax.broadcasted_iota(jnp.int32, (128, cols), 0)
    spread = ((col >= lane * head) & (col < (lane + 1) * head)).astype(F32).astype(BF16)
    query = q_ref[...].astype(F32)
    half = half_ref[0:1, :]
    frame = frame_ref[0]
    keyvals = (k0, k1, k2, k3, k4)
    masked, valids = [], []
    for index, ref in enumerate(keyvals):
        offset = index - WMAX
        score = dot2(query * ref[:, :cols].astype(F32), gather) / (float(head) ** 0.5)
        target = frame + offset
        inside = ((target >= 0) & (target < frames)).astype(F32)
        valid = (inside * (half >= abs(offset)).astype(F32)) > 0.5
        valids.append(valid)
        masked.append(jnp.where(valid, score, -1e30))
    top = masked[0]
    for value in masked[1:]:
        top = jnp.maximum(top, value)
    expo = [jnp.where(valid, jnp.exp(value - top), 0.0) for valid, value in zip(valids, masked)]
    total = expo[0]
    for value in expo[1:]:
        total = total + value
    out = jnp.zeros((rows, cols), F32)
    for value, ref in zip(expo, keyvals):
        out = out + dot2(value / total, spread) * ref[:, cols:].astype(F32)
    out_ref[...] = out.astype(BF16)


def mlp_kernel(
    head, hidden, ylo_ref, att_ref, tok_ref, mod_ref, oa_ref, ob_ref, m0, m1, m2, m3, resid_ref, part_ref
):
    groups = att_ref.shape[0]
    ylo = ylo_ref[0]
    rows = tok_ref.shape[0]
    attn = jnp.zeros(tok_ref.shape, F32)
    for group in range(groups):
        for far in range(2):
            line = ylo if far == 0 else 1 - ylo
            for core, ref in enumerate((oa_ref, ob_ref)):
                slot = far * 2 + core
                block = att_ref[group, :, slot * head : (slot + 1) * head]
                attn = attn + jnp.dot(block, ref[group, line], preferred_element_type=F32)
    resid = (tok_ref[...].astype(F32) + mod_ref[2:3, :] * attn).astype(BF16)
    resid_ref[...] = resid
    normed = normalise(resid.astype(F32), mod_ref[3:4, :], mod_ref[4:5, :])
    total = jnp.zeros(tok_ref.shape, F32)
    for ref in (m0, m1, m2, m3):
        wide = lax.dot_general(
            normed, ref[hidden:, :], (((1,), (1,)), ((), ())), preferred_element_type=F32
        )
        active = jax.nn.gelu(wide, approximate=True).astype(BF16)
        total = total + jnp.dot(active, ref[:hidden, :], preferred_element_type=F32)
    part_ref[...] = total.astype(BF16)


def call(kernel, outs, smem, *args):
    specs = [pl.BlockSpec(memory_space=pltpu.SMEM)] * smem
    specs += [pl.BlockSpec(memory_space=pltpu.VMEM)] * (len(args) - smem)
    return pl.pallas_call(
        kernel,
        out_shape=outs,
        in_specs=specs,
        out_specs=jax.tree.map(lambda _: pl.BlockSpec(memory_space=pltpu.VMEM), outs),
        compiler_params=PARAMS,
    )(*args)


def per_device(
    latents,
    fresh_noise,
    levels,
    modulation,
    head_map,
    window,
    qkv_weight,
    out_weight,
    fc1_weight,
    fc2_weight,
):
    tokens, width = latents.shape[1:]
    level_count = modulation.shape[0]
    head = out_weight.shape[0]
    hidden = fc2_weight.shape[0]
    slots = lax.axis_size(SLOTS)
    slot = lax.axis_index(SLOTS)
    ylo = lax.axis_index("ylo").astype(jnp.int32)
    across = lax.axis_index("x")
    around = lax.axis_size("x")

    def slid(value, steps):
        return lax.ppermute(value, SLOTS, [(s, (s + steps) % slots) for s in range(slots)])

    half = jnp.sum(jnp.where(jnp.arange(window.shape[0]) == head_map[0], window, 0))
    own_w = jnp.concatenate(
        [qkv_weight, jnp.broadcast_to(half.astype(BF16), (16, qkv_weight.shape[1]))], axis=0
    )
    near_w = lax.ppermute(own_w, "ylo", SWAP)
    core_w = lax.ppermute(own_w, "core", SWAP)
    payload = jnp.concatenate(
        [latents[0], jnp.broadcast_to(levels.astype(BF16)[:, None], (16, width))], axis=0
    )
    moved = slid(payload, 1)
    far_w = lax.ppermute(core_w, ("yhi", "ylo"), FAR_Y)
    out_a = lax.all_gather(out_weight, ("x", "ylo"), axis=0, tiled=False).reshape(
        around, 2, head, width
    )
    own_m = jnp.concatenate([fc2_weight, fc1_weight.T], axis=0)
    core_m = lax.ppermute(own_m, "core", SWAP)

    tok = lax.all_gather(moved[:tokens], "x", axis=0, tiled=True)
    level = moved[tokens, 0].astype(jnp.int32)
    picked = jnp.sum(
        jnp.where(jnp.arange(level_count)[:, None, None] == level, modulation, 0.0), axis=0
    )
    rows = tok.shape[0]
    cols = 4 * head
    query, keyval, halfs = call(
        lambda *refs: qkv_kernel(head, width, *refs),
        (
            jax.ShapeDtypeStruct((rows, cols), BF16),
            jax.ShapeDtypeStruct((rows, 2 * cols), BF16),
            jax.ShapeDtypeStruct((16, 128), F32),
        ),
        0,
        tok,
        picked,
        own_w,
        core_w,
        near_w,
        far_w,
    )
    near_m = lax.ppermute(own_m, "ylo", SWAP)
    far_m = lax.ppermute(core_m, ("yhi", "ylo"), FAR_Y)
    arrived = [slid(keyval, 2), slid(keyval, 1), keyval, slid(keyval, -1), slid(keyval, -2)]
    out_b = lax.ppermute(out_a, "core", SWAP)
    frame = jnp.where(slot == 0, slots - 1, slot - 1).astype(jnp.int32)
    attended = call(
        lambda *refs: attention_kernel(head, slots, *refs),
        jax.ShapeDtypeStruct((rows, cols), BF16),
        1,
        frame[None],
        halfs,
        query,
        *arrived,
    )
    att = lax.all_gather(attended, "x", axis=0, tiled=False)
    resid, part = call(
        lambda *refs: mlp_kernel(head, hidden, *refs),
        (jax.ShapeDtypeStruct((rows, width), BF16), jax.ShapeDtypeStruct((rows, width), BF16)),
        1,
        ylo[None],
        att,
        tok,
        picked,
        out_a,
        out_b,
        own_m,
        core_m,
        near_m,
        far_m,
    )
    parts = lax.all_to_all(part, "x", 0, 0, tiled=True).reshape(around, tokens, width)
    mlp = jnp.sum(parts.astype(F32), axis=0)
    mine = lax.dynamic_slice_in_dim(resid, across * tokens, tokens, 0)
    block_out = (mine.astype(F32) + picked[5] * mlp).astype(BF16)
    return jnp.where(slot == 0, fresh_noise, block_out)[None]


def solution(mesh):
    split = Mesh(mesh.devices.reshape(2, 16, 4, 2, 2), ("yhi", "z", "x", "ylo", "core"))
    mp = ("x", "ylo", "core")
    in_specs = (
        P(SLOTS, mp, None),
        P(mp, None),
        P(SLOTS),
        P(),
        P(mp),
        P(),
        P(None, mp),
        P(mp, None),
        P(None, mp),
        P(mp, None),
    )
    return jax.shard_map(
        per_device, mesh=split, in_specs=in_specs, out_specs=P(SLOTS, mp, None), check_vma=False
    )
```

```python
import jax
import jax.numpy as jnp
from jax import lax
from jax.experimental import pallas as pl
from jax.experimental.pallas import tpu as pltpu
from jax.sharding import Mesh
from jax.sharding import PartitionSpec as P

WMAX = 2
MEGA = 1024 * 1024
BF16, F32 = jnp.bfloat16, jnp.float32
SLOTS = ("yhi", "z")
SWAP = [(0, 1), (1, 0)]
FAR_Y = [(0, 3), (3, 0), (1, 2), (2, 1)]
FAR = [(2 * y + core, 2 * to + 1 - core) for y, to in FAR_Y for core in range(2)]


def normalise(floats, shift, scale):
    center = jnp.mean(floats, axis=-1, keepdims=True)
    spread = jnp.mean((floats - center) ** 2, axis=-1, keepdims=True)
    return ((floats - center) * lax.rsqrt(spread + 1e-06) * (1.0 + scale) + shift).astype(BF16)


def start_all(pairs, sems):
    copies = [pltpu.make_async_copy(src, dst, sems.at[i]) for i, (src, dst) in enumerate(pairs)]
    for copy in copies:
        copy.start()
    return copies


def prepare_kernel(
    levels_ref, map_ref, window_ref, latents_ref, qkv_ref, out_ref, fc1_ref, fc2_ref,
    tok_ref, packed_ref, mlp_ref, latents_here, qkv_here, out_here, sems,
):
    tokens, width = latents_ref.shape
    lines = qkv_ref.shape[0]
    hidden = fc2_ref.shape[0]
    copies = start_all(
        [
            (latents_ref, latents_here),
            (qkv_ref, qkv_here),
            (out_ref, out_here),
            (fc2_ref, mlp_ref.at[0:hidden]),
            (fc1_ref, mlp_ref.at[hidden : 2 * hidden]),
        ],
        sems,
    )
    tok_ref[tokens:, :] = jnp.full((tok_ref.shape[0] - tokens, width), levels_ref[0].astype(F32)).astype(BF16)
    half = jnp.full((8, width), window_ref[map_ref[0]].astype(F32))
    packed_ref[lines : lines + 8, :] = half.astype(BF16)
    copies[0].wait()
    tok_ref[0:tokens, :] = latents_here[...]
    copies[1].wait()
    packed_ref[0:lines, :] = qkv_here[...]
    copies[2].wait()
    packed_ref[lines + 8 : lines + 8 + out_ref.shape[0], :] = out_here[...]
    packed_ref[lines + 8 + out_ref.shape[0] :, :] = jnp.zeros((8, width), BF16)
    copies[3].wait()
    copies[4].wait()


def qkv_kernel(
    head, t0, t1, t2, t3, mods_ref, w0, w1, w2, w3, q_ref, kv_ref, half_ref, mod_ref,
    q_here, half_here, mod_here, sems,
):
    tokens, width = t1.shape
    level = t0[tokens:, :].astype(F32)[0:1, :]
    lines = lax.broadcasted_iota(jnp.int32, (mods_ref.shape[1], width), 0).astype(F32)
    chosen = lines == level
    picked = [
        jnp.sum(jnp.where(chosen, mods_ref[index], 0.0), axis=0, keepdims=True)
        for index in range(mods_ref.shape[0])
    ]
    mod_here[...] = jnp.concatenate(picked + picked[:2], axis=0)
    blocks = (t0[0:tokens, :], t1[...], t2[...], t3[...])
    normed = jnp.concatenate(
        [normalise(block.astype(F32), picked[0], picked[1]) for block in blocks], axis=0
    )
    queries, keys, values = [], [], []
    lane = lax.broadcasted_iota(jnp.int32, half_here.shape, 1)
    half = jnp.zeros(half_here.shape, F32)
    for slot, weight in enumerate((w0, w1, w2, w3)):
        part = lax.dot_general(
            normed, weight[0 : 3 * head, :], (((1,), (1,)), ((), ())), preferred_element_type=F32
        )
        queries.append(part[:, :head])
        keys.append(part[:, head : 2 * head])
        values.append(part[:, 2 * head :])
        mark = weight[3 * head - 8 : 3 * head + 8, 0:128].astype(F32)[8:16]
        half = jnp.where(lane == slot, mark, half)
    half_here[...] = half
    q_here[...] = jnp.concatenate(queries, axis=1).astype(BF16)
    copies = start_all([(mod_here, mod_ref), (half_here, half_ref), (q_here, q_ref)], sems)
    kv_ref[...] = jnp.concatenate(keys + values, axis=1).astype(BF16)
    for copy in copies:
        copy.wait()


def attention_kernel(
    head, frames, frame_ref, x_ref, half_ref, q_ref, k0, k1, k2, k3, k4, own_o, w1, w2, w3, out_ref,
    half_here, q_here, own_here, sems,
):
    rows, cols = q_ref.shape
    first = 3 * head + 8
    copies = start_all(
        [(half_ref, half_here), (q_ref, q_here), (own_o, own_here)],
        sems,
    )
    col = lax.broadcasted_iota(jnp.int32, (cols, 128), 0)
    lane = lax.broadcasted_iota(jnp.int32, (cols, 128), 1)
    gather = ((col >= lane * head) & (col < (lane + 1) * head)).astype(F32).astype(BF16)
    col = lax.broadcasted_iota(jnp.int32, (128, cols), 1)
    lane = lax.broadcasted_iota(jnp.int32, (128, cols), 0)
    spread = ((col >= lane * head) & (col < (lane + 1) * head)).astype(F32).astype(BF16)
    copies[0].wait()
    copies[1].wait()
    query = q_here[...].astype(F32)
    half = half_here[0:1, :]
    frame = frame_ref[0]
    keyvals = (k0, k1, k2, k3, k4)
    masked, valids = [], []
    for index, ref in enumerate(keyvals):
        offset = index - WMAX
        products = (query * ref[:, :cols].astype(F32)).astype(BF16)
        score = jnp.dot(products, gather, preferred_element_type=F32) / (float(head) ** 0.5)
        target = frame + offset
        inside = ((target >= 0) & (target < frames)).astype(F32)
        valid = (inside * (half >= abs(offset)).astype(F32)) > 0.5
        valids.append(valid)
        masked.append(jnp.where(valid, score, -1e30))
    top = masked[0]
    for value in masked[1:]:
        top = jnp.maximum(top, value)
    expo = [jnp.where(valid, jnp.exp(value - top), 0.0) for valid, value in zip(valids, masked)]
    total = expo[0]
    for value in expo[1:]:
        total = total + value
    mixed = jnp.zeros((rows, cols), F32)
    for value, ref in zip(expo, keyvals):
        wide = jnp.dot((value / total).astype(BF16), spread, preferred_element_type=F32)
        mixed = mixed + wide * ref[:, cols:].astype(F32)
    mixed = mixed.astype(BF16)
    for copy in copies[2:]:
        copy.wait()
    weight = [own_here[...].astype(F32)]
    weight += [ref[first : first + head, :].astype(F32) for ref in (w1, w2, w3)]
    weight = jnp.concatenate(weight, axis=0).astype(BF16)
    attn = jnp.dot(mixed, weight, preferred_element_type=F32).astype(BF16)
    tokens = rows // 4
    for block in range(4):
        place = lax.rem(x_ref[0] + 4 - block, 4) * tokens
        out_ref[pl.ds(pl.multiple_of(place, 16), tokens), :] = attn[block * tokens : (block + 1) * tokens]


def total_of(parts_ref, tokens):
    total = parts_ref[0:tokens, :].astype(F32)
    for block in range(1, parts_ref.shape[0] // tokens):
        total = total + parts_ref[block * tokens : (block + 1) * tokens, :].astype(F32)
    return total


def resid_kernel(parts_ref, tok_ref, mod_ref, resid_ref, normed_ref):
    tokens = resid_ref.shape[0]
    attn = total_of(parts_ref, tokens)
    resid = (tok_ref[0:tokens, :].astype(F32) + mod_ref[2:3, :] * attn).astype(BF16)
    resid_ref[...] = resid
    normed_ref[...] = normalise(resid.astype(F32), mod_ref[3:4, :], mod_ref[4:5, :])


def mlp_kernel(hidden, normed_ref, m0, m1, m2, m3, part_ref):
    normed = normed_ref[...]
    total = jnp.zeros(normed.shape, F32)
    for ref in (m0, m1, m2, m3):
        wide = lax.dot_general(
            normed, ref[hidden:, :], (((1,), (1,)), ((), ())), preferred_element_type=F32
        )
        active = jax.nn.gelu(wide, approximate=True).astype(BF16)
        total = total + jnp.dot(active, ref[:hidden, :], preferred_element_type=F32)
    part_ref[...] = total.astype(BF16)


def final_kernel(slot_ref, parts_ref, resid_ref, mod_ref, fresh_ref, out_ref):
    tokens = resid_ref.shape[0]
    mlp = total_of(parts_ref, tokens)
    block_out = (resid_ref[...].astype(F32) + mod_ref[5:6, :] * mlp).astype(BF16)
    out_ref[...] = jnp.where(slot_ref[0] == 0, fresh_ref[...].astype(F32), block_out.astype(F32)).astype(BF16)


SPECS = {
    "s": pl.BlockSpec(memory_space=pltpu.SMEM),
    "v": pl.BlockSpec(memory_space=pltpu.VMEM),
    "a": pl.BlockSpec(memory_space=pltpu.HBM),
}


def call(kernel, outs, kinds, *args, scratch=(), flops=0, limit=16):
    ins, back = ([SPECS[kind] for kind in part] for part in kinds.split(">"))
    args = [
        pltpu.with_memory_space_constraint(arg, pltpu.HBM) if kind == "a" else arg
        for arg, kind in zip(args, kinds)
    ]
    return pl.pallas_call(
        kernel,
        out_shape=outs,
        in_specs=ins,
        out_specs=tuple(back) if isinstance(outs, tuple) else back[0],
        scratch_shapes=scratch,
        compiler_params=pltpu.CompilerParams(vmem_limit_bytes=limit * MEGA),
        cost_estimate=pl.CostEstimate(flops=flops, bytes_accessed=1 << 20, transcendentals=0),
    )(*args)


def per_device(
    latents,
    fresh_noise,
    levels,
    modulation,
    head_map,
    window,
    qkv_weight,
    out_weight,
    fc1_weight,
    fc2_weight,
):
    tokens, width = latents.shape[1:]
    head = out_weight.shape[0]
    hidden = fc2_weight.shape[0]
    slots = lax.axis_size(SLOTS)
    slot = lax.axis_index(SLOTS)
    around = lax.axis_size("x")

    def slid(value, steps):
        return lax.ppermute(value, SLOTS, [(s, (s + steps) % slots) for s in range(slots)])

    def shape(*dims, dtype=BF16):
        return jax.ShapeDtypeStruct(dims, dtype)

    payload, own_w, own_m = call(
        prepare_kernel,
        (shape(tokens + 16, width), shape(4 * head + 16, width), shape(2 * hidden, width)),
        "sssaaaaa>vvv",
        levels,
        head_map,
        window,
        latents[0],
        qkv_weight.T,
        out_weight,
        fc1_weight.T,
        fc2_weight,
        scratch=[
            pltpu.VMEM((tokens, width), BF16),
            pltpu.VMEM((3 * head, width), BF16),
            pltpu.VMEM((head, width), BF16),
            pltpu.SemaphoreType.DMA((5,)),
        ],
    )
    def come(value, back):
        pairs = [
            (s * around + x, (s + 1) % slots * around + (x + back) % around)
            for s in range(slots)
            for x in range(around)
        ]
        return lax.ppermute(value, SLOTS + ("x",), pairs)

    core_w = lax.ppermute(own_w, "core", SWAP)
    near_w = lax.ppermute(own_w, "ylo", SWAP)
    far_w = lax.ppermute(own_w, ("yhi", "ylo", "core"), FAR)
    toks = [come(payload if back == 0 else latents[0], back) for back in range(around)]

    rows = around * tokens
    cols = 4 * head
    query, keyval, halfs, mod = call(
        lambda *refs: qkv_kernel(head, *refs),
        (
            pltpu.HBM((rows, cols), BF16),
            shape(rows, 2 * cols),
            pltpu.HBM((8, 128), F32),
            pltpu.HBM((8, width), F32),
        ),
        "vvvvvvvvv>avaa",
        *toks,
        modulation.transpose(1, 0, 2),
        own_w,
        core_w,
        near_w,
        far_w,
        scratch=[
            pltpu.VMEM((rows, cols), BF16),
            pltpu.VMEM((8, 128), F32),
            pltpu.VMEM((8, width), F32),
            pltpu.SemaphoreType.DMA((3,)),
        ],
    )
    arrived = [slid(keyval, 2), slid(keyval, 1), slid(keyval, -1), slid(keyval, -2)]
    own_m, keyval = lax.optimization_barrier((own_m, keyval))
    core_m = lax.ppermute(own_m, "core", SWAP)
    near_m = lax.ppermute(own_m, "ylo", SWAP)
    far_m = lax.ppermute(own_m, ("yhi", "ylo", "core"), FAR)
    frame = jnp.where(slot == 0, slots - 1, slot - 1).astype(jnp.int32)
    attended = call(
        lambda *refs: attention_kernel(head, slots, *refs),
        shape(rows, width),
        "ssaavvvvvavvv>v",
        frame[None],
        lax.axis_index("x").astype(jnp.int32)[None],
        halfs,
        query,
        *arrived[:2],
        keyval,
        *arrived[2:],
        out_weight,
        core_w,
        near_w,
        far_w,
        scratch=[
            pltpu.VMEM((8, 128), F32),
            pltpu.VMEM((rows, cols), BF16),
            pltpu.VMEM((head, width), BF16),
            pltpu.SemaphoreType.DMA((3,)),
        ],
        flops=100 * 10**9,
    )
    parts = lax.all_to_all(attended, "x", 0, 0, tiled=True)
    resid, normed = call(
        resid_kernel, (shape(tokens, width), shape(tokens, width)), "vvv>vv", parts, toks[0], mod
    )
    part = call(
        lambda *refs: mlp_kernel(hidden, *refs),
        shape(rows, width),
        "vvvvv>v",
        lax.all_gather(normed, "x", axis=0, tiled=True),
        own_m,
        core_m,
        near_m,
        far_m,
    )
    parts = lax.all_to_all(part, "x", 0, 0, tiled=True)
    return call(
        final_kernel,
        shape(tokens, width),
        "svvvv>v",
        slot[None].astype(jnp.int32),
        parts,
        resid,
        mod,
        fresh_noise,
    )[None]


def solution(mesh):
    split = Mesh(mesh.devices.reshape(2, 16, 4, 2, 2), ("yhi", "z", "x", "ylo", "core"))
    mp = ("x", "ylo", "core")
    in_specs = (
        P(SLOTS, mp, None),
        P(mp, None),
        P(SLOTS),
        P(),
        P(mp),
        P(),
        P(None, mp),
        P(mp, None),
        P(None, mp),
        P(mp, None),
    )
    return jax.shard_map(
        per_device, mesh=split, in_specs=in_specs, out_specs=P(SLOTS, mp, None), check_vma=False
    )
```

```python
import jax
import jax.numpy as jnp
from jax import lax
from jax.experimental import pallas as pl
from jax.experimental.pallas import tpu as pltpu
from jax.sharding import Mesh
from jax.sharding import PartitionSpec as P

MEGA = 1024 * 1024
BF16, F32 = jnp.bfloat16, jnp.float32
SLOTS = ("yhi", "z")
SWAP = [(0, 1), (1, 0)]
FAR_Y = [(0, 3), (3, 0), (1, 2), (2, 1)]
FAR = [(2 * y + core, 2 * to + 1 - core) for y, to in FAR_Y for core in range(2)]


def normalise(floats, shift, scale):
    center = jnp.mean(floats, axis=-1, keepdims=True)
    spread = jnp.mean((floats - center) ** 2, axis=-1, keepdims=True)
    return ((floats - center) * lax.rsqrt(spread + 1e-06) * (1.0 + scale) + shift).astype(BF16)


def start_all(pairs, sems):
    copies = [pltpu.make_async_copy(src, dst, sems.at[i]) for i, (src, dst) in enumerate(pairs)]
    for copy in copies:
        copy.start()
    return copies


def prepare_kernel(
    levels_ref, map_ref, window_ref, latents_ref, mods_ref, qkv_ref, out_ref,
    tok_ref, packed_ref, window_here, latents_here, mods_here, qkv_here, out_here, sems,
):
    tokens, width = latents_ref.shape
    lines, rows = qkv_ref.shape[0], out_ref.shape[0]
    level = levels_ref[0]
    group = pl.multiple_of(level // 8 * 8, 8)
    copies = start_all(
        [
            (window_ref, window_here),
            (mods_ref.at[:, pl.ds(group, 8), :], mods_here),
            (latents_ref, latents_here),
            (qkv_ref, qkv_here),
            (out_ref, out_here),
        ],
        sems,
    )
    packed_ref[lines + 8 + rows :, :] = jnp.zeros((8, width), BF16)
    copies[0].wait()
    half = jnp.full((8, width), window_here[map_ref[0]].astype(F32))
    packed_ref[lines : lines + 8, :] = half.astype(BF16)
    copies[1].wait()
    chosen = lax.broadcasted_iota(jnp.int32, (8, width), 0) == level - group
    picked = [
        jnp.sum(jnp.where(chosen, mods_here[index], 0.0), axis=0, keepdims=True)
        for index in range(mods_here.shape[0])
    ]
    rest = jnp.concatenate(picked + picked[:2], axis=0)
    terms = []
    for _ in range(3):
        term = rest.astype(BF16).astype(F32)
        terms.append(term)
        rest = rest - term
    tok_ref[tokens:, :] = jnp.concatenate(terms + terms[:1], axis=0).astype(BF16)
    copies[2].wait()
    tok_ref[0:tokens, :] = latents_here[...]
    copies[3].wait()
    packed_ref[0:lines, :] = qkv_here[...]
    copies[4].wait()
    packed_ref[lines + 8 : lines + 8 + rows, :] = out_here[...]


def mod_of(tok_ref, tokens):
    terms = tok_ref[tokens:, :].astype(F32)
    return terms[0:8] + (terms[8:16] + terms[16:24])


def norm_kernel(tok_ref, normed_ref):
    tokens = normed_ref.shape[0]
    mod = mod_of(tok_ref, tokens)
    normed_ref[...] = normalise(tok_ref[0:tokens, :].astype(F32), mod[0:1, :], mod[1:2, :])


def qkv_kernel(
    head, t0, t1, t2, t3, w0, w1, w2, w3, fc1_ref, fc2_ref, q_ref, kv_ref, half_ref, mlp_ref,
    q_here, half_here, sems,
):
    hidden = fc2_ref.shape[0]
    weights = start_all(
        [(fc2_ref, mlp_ref.at[0:hidden]), (fc1_ref, mlp_ref.at[hidden : 2 * hidden])], sems
    )
    normed = jnp.concatenate([block[...] for block in (t0, t1, t2, t3)], axis=0)
    queries, keys, values = [], [], []
    lane = lax.broadcasted_iota(jnp.int32, half_here.shape, 1)
    half = jnp.zeros(half_here.shape, F32)
    for slot, weight in enumerate((w0, w1, w2, w3)):
        part = lax.dot_general(
            normed, weight[0 : 3 * head, :], (((1,), (1,)), ((), ())), preferred_element_type=F32
        )
        queries.append(part[:, :head])
        keys.append(part[:, head : 2 * head])
        values.append(part[:, 2 * head :])
        mark = weight[3 * head - 8 : 3 * head + 8, 0:128].astype(F32)[8:16]
        half = jnp.where(lane == slot, mark, half)
    half_here[...] = half
    q_here[...] = jnp.concatenate(queries, axis=1).astype(BF16)
    copies = weights + start_all([(half_here, half_ref), (q_here, q_ref)], sems.at[2:4])
    kv_ref[...] = jnp.concatenate(keys + values, axis=1).astype(BF16)
    for copy in copies:
        copy.wait()


def attention_kernel(
    head, slots, slot_ref, x_ref, half_ref, q_ref, k0, k1, k2, k3, k4, own_o, w1, w2, w3, out_ref,
    half_here, q_here, own_here, sems,
):
    rows, cols = q_ref.shape
    first = 3 * head + 8
    copies = start_all(
        [(half_ref, half_here), (q_ref, q_here), (own_o, own_here)],
        sems,
    )
    col = lax.broadcasted_iota(jnp.int32, (cols, 128), 0)
    lane = lax.broadcasted_iota(jnp.int32, (cols, 128), 1)
    gather = ((col >= lane * head) & (col < (lane + 1) * head)).astype(F32).astype(BF16)
    col = lax.broadcasted_iota(jnp.int32, (128, cols), 1)
    lane = lax.broadcasted_iota(jnp.int32, (128, cols), 0)
    spread = ((col >= lane * head) & (col < (lane + 1) * head)).astype(F32).astype(BF16)
    copies[0].wait()
    copies[1].wait()
    query = q_here[...].astype(F32)
    half = half_here[0:1, :]
    place = slot_ref[0]
    frame = lax.rem(place + slots - 1, slots)
    odd, upper = place & 1, place & 2
    keyvals = (k0, k1, k2, k3, k4)
    offsets = (0, 1 - 2 * odd, 2 * odd - 1, 2 - 2 * upper, 2 * upper - 2)
    products = [(query * ref[:, :cols].astype(F32)).astype(BF16) for ref in keyvals]
    scores = jnp.dot(jnp.concatenate(products, axis=0), gather, preferred_element_type=F32)
    masked, valids = [], []
    for index, (offset, reach) in enumerate(zip(offsets, (0, 1, 1, 2, 2))):
        score = scores[index * rows : (index + 1) * rows] / (float(head) ** 0.5)
        target = frame + offset
        inside = ((target >= 0) & (target < slots)).astype(F32)
        valid = (inside * (half >= reach).astype(F32)) > 0.5
        valids.append(valid)
        masked.append(jnp.where(valid, score, -1e30))
    top = masked[0]
    for value in masked[1:]:
        top = jnp.maximum(top, value)
    expo = [jnp.where(valid, jnp.exp(value - top), 0.0) for valid, value in zip(valids, masked)]
    total = expo[0]
    for value in expo[1:]:
        total = total + value
    probs = jnp.concatenate([(value / total).astype(BF16) for value in expo], axis=0)
    wide = jnp.dot(probs, spread, preferred_element_type=F32)
    mixed = jnp.zeros((rows, cols), F32)
    for index, ref in enumerate(keyvals):
        mixed = mixed + wide[index * rows : (index + 1) * rows] * ref[:, cols:].astype(F32)
    mixed = mixed.astype(BF16)
    for copy in copies[2:]:
        copy.wait()
    weight = [own_here[...].astype(F32)]
    weight += [ref[first : first + head, :].astype(F32) for ref in (w1, w2, w3)]
    weight = jnp.concatenate(weight, axis=0).astype(BF16)
    attn = jnp.dot(mixed, weight, preferred_element_type=F32).astype(BF16)
    tokens = rows // 4
    for block in range(4):
        place = (x_ref[0] ^ block) * tokens
        out_ref[pl.ds(pl.multiple_of(place, 16), tokens), :] = attn[block * tokens : (block + 1) * tokens]


def total_of(parts_ref, tokens):
    total = parts_ref[0:tokens, :].astype(F32)
    for block in range(1, parts_ref.shape[0] // tokens):
        total = total + parts_ref[block * tokens : (block + 1) * tokens, :].astype(F32)
    return total


def resid_kernel(parts_ref, tok_ref, resid_ref, normed_ref):
    tokens = resid_ref.shape[0]
    mod = mod_of(tok_ref, tokens)
    attn = total_of(parts_ref, tokens)
    resid = (tok_ref[0:tokens, :].astype(F32) + mod[2:3, :] * attn).astype(BF16)
    resid_ref[...] = resid
    normed_ref[...] = normalise(resid.astype(F32), mod[3:4, :], mod[4:5, :])


def mlp_kernel(hidden, normed_ref, m0, m1, m2, m3, part_ref):
    refs = (m0, m1, m2, m3)
    first = jnp.concatenate([ref[hidden:, :] for ref in refs], axis=0)
    wide = lax.dot_general(
        normed_ref[...], first, (((1,), (1,)), ((), ())), preferred_element_type=F32
    )
    active = jax.nn.gelu(wide, approximate=True).astype(BF16)
    second = jnp.concatenate([ref[:hidden, :] for ref in refs], axis=0)
    part_ref[...] = jnp.dot(active, second, preferred_element_type=F32).astype(BF16)


def final_kernel(slot_ref, parts_ref, resid_ref, tok_ref, fresh_ref, out_ref):
    tokens = resid_ref.shape[0]
    mod = mod_of(tok_ref, tokens)
    mlp = total_of(parts_ref, tokens)
    block_out = (resid_ref[...].astype(F32) + mod[5:6, :] * mlp).astype(BF16)
    out_ref[...] = jnp.where(slot_ref[0] == 0, fresh_ref[...].astype(F32), block_out.astype(F32)).astype(BF16)


SPECS = {
    "s": pl.BlockSpec(memory_space=pltpu.SMEM),
    "v": pl.BlockSpec(memory_space=pltpu.VMEM),
    "a": pl.BlockSpec(memory_space=pltpu.HBM),
}


def call(kernel, outs, kinds, *args, scratch=(), flops=0, limit=16):
    ins, back = ([SPECS[kind] for kind in part] for part in kinds.split(">"))
    args = [
        pltpu.with_memory_space_constraint(arg, pltpu.HBM) if kind == "a" else arg
        for arg, kind in zip(args, kinds)
    ]
    return pl.pallas_call(
        kernel,
        out_shape=outs,
        in_specs=ins,
        out_specs=tuple(back) if isinstance(outs, tuple) else back[0],
        scratch_shapes=scratch,
        compiler_params=pltpu.CompilerParams(vmem_limit_bytes=limit * MEGA),
        cost_estimate=pl.CostEstimate(flops=flops, bytes_accessed=1 << 20, transcendentals=0),
    )(*args)


def per_device(
    latents,
    fresh_noise,
    levels,
    modulation,
    head_map,
    window,
    qkv_weight,
    out_weight,
    fc1_weight,
    fc2_weight,
):
    tokens, width = latents.shape[1:]
    head = out_weight.shape[0]
    hidden = fc2_weight.shape[0]
    slots = lax.axis_size(SLOTS)
    slot = lax.axis_index(SLOTS)
    around = lax.axis_size("x")

    def shape(*dims, dtype=BF16):
        return jax.ShapeDtypeStruct(dims, dtype)

    payload, own_w = call(
        prepare_kernel,
        (shape(tokens + 32, width), shape(4 * head + 16, width)),
        "ssaaaaa>vv",
        levels,
        head_map,
        window,
        latents[0],
        modulation.transpose(1, 0, 2),
        qkv_weight.T,
        out_weight,
        scratch=[
            pltpu.SMEM(window.shape, jnp.int32),
            pltpu.VMEM((tokens, width), BF16),
            pltpu.VMEM((modulation.shape[1], 8, width), F32),
            pltpu.VMEM((3 * head, width), BF16),
            pltpu.VMEM((head, width), BF16),
            pltpu.SemaphoreType.DMA((5,)),
        ],
    )
    moved = lax.ppermute(payload, SLOTS, [(s, (s + 1) % slots) for s in range(slots)])
    core_w = lax.ppermute(own_w, "core", SWAP)
    near_w = lax.ppermute(own_w, "ylo", SWAP)
    far_w = lax.ppermute(own_w, ("yhi", "ylo", "core"), FAR)
    normed = call(norm_kernel, shape(tokens, width), "v>v", moved, flops=100 * 10**9)
    toks = [normed]
    toks += [lax.ppermute(normed, "x", [(x, x ^ j) for x in range(around)]) for j in range(1, around)]

    rows = around * tokens
    cols = 4 * head
    query, keyval, halfs, own_m = call(
        lambda *refs: qkv_kernel(head, *refs),
        (
            pltpu.HBM((rows, cols), BF16),
            shape(rows, 2 * cols),
            pltpu.HBM((8, 128), F32),
            shape(2 * hidden, width),
        ),
        "vvvvvvvvaa>avav",
        *toks,
        own_w,
        core_w,
        near_w,
        far_w,
        fc1_weight.T,
        fc2_weight,
        scratch=[
            pltpu.VMEM((rows, cols), BF16),
            pltpu.VMEM((8, 128), F32),
            pltpu.SemaphoreType.DMA((4,)),
        ],
    )
    ones = [(s, s ^ 1) for s in range(slots)]
    others = [(s, (((s - 1) ^ 1) + 1) % slots) for s in range(1, slots + 1)]
    others = [(s % slots, to) for s, to in others]
    twos = [(s, s ^ 2) for s in range(slots)]
    rest = [(s % slots, (((s - 2) ^ 2) + 2) % slots) for s in range(2, slots + 2)]
    arrived = [lax.ppermute(keyval, SLOTS, pairs) for pairs in (ones, others, twos, rest)]
    near_m = lax.ppermute(own_m, "ylo", SWAP)
    far_m = lax.ppermute(own_m, ("yhi", "ylo", "core"), FAR)
    core_m = lax.ppermute(lax.optimization_barrier((own_m, arrived[2]))[0], "core", SWAP)
    attended = call(
        lambda *refs: attention_kernel(head, slots, *refs),
        shape(rows, width),
        "ssaavvvvvavvv>v",
        slot.astype(jnp.int32)[None],
        lax.axis_index("x").astype(jnp.int32)[None],
        halfs,
        query,
        keyval,
        *arrived,
        out_weight,
        core_w,
        near_w,
        far_w,
        scratch=[
            pltpu.VMEM((8, 128), F32),
            pltpu.VMEM((rows, cols), BF16),
            pltpu.VMEM((head, width), BF16),
            pltpu.SemaphoreType.DMA((3,)),
        ],
        flops=100 * 10**9,
    )
    parts = lax.all_to_all(attended, "x", 0, 0, tiled=True)
    resid, normed = call(
        resid_kernel, (shape(tokens, width), shape(tokens, width)), "vv>vv", parts, moved
    )
    part = call(
        lambda *refs: mlp_kernel(hidden, *refs),
        shape(rows, width),
        "vvvvv>v",
        lax.all_gather(normed, "x", axis=0, tiled=True),
        own_m,
        core_m,
        near_m,
        far_m,
    )
    parts = lax.all_to_all(part, "x", 0, 0, tiled=True)
    return call(
        final_kernel,
        shape(tokens, width),
        "svvvv>v",
        slot[None].astype(jnp.int32),
        parts,
        resid,
        moved,
        fresh_noise,
    )[None]


def solution(mesh):
    split = Mesh(mesh.devices.reshape(2, 16, 4, 2, 2), ("yhi", "z", "x", "ylo", "core"))
    mp = ("x", "ylo", "core")
    in_specs = (
        P(SLOTS, mp, None),
        P(mp, None),
        P(SLOTS),
        P(),
        P(mp),
        P(),
        P(None, mp),
        P(mp, None),
        P(None, mp),
        P(mp, None),
    )
    return jax.shard_map(
        per_device, mesh=split, in_specs=in_specs, out_specs=P(SLOTS, mp, None), check_vma=False
    )
```

```python
import jax
import jax.numpy as jnp
from jax import lax
from jax.experimental import pallas as pl
from jax.experimental.pallas import tpu as pltpu
from jax.sharding import Mesh
from jax.sharding import PartitionSpec as P

MEGA = 1024 * 1024
BF16, F32 = jnp.bfloat16, jnp.float32
SLOTS = ("yhi", "z")
SWAP = [(0, 1), (1, 0)]
FAR_Y = [(0, 3), (3, 0), (1, 2), (2, 1)]
FAR = [(2 * y + core, 2 * to + 1 - core) for y, to in FAR_Y for core in range(2)]


def normalise(floats, shift, scale):
    center = jnp.mean(floats, axis=-1, keepdims=True)
    spread = jnp.mean((floats - center) ** 2, axis=-1, keepdims=True)
    return ((floats - center) * lax.rsqrt(spread + 1e-06) * (1.0 + scale) + shift).astype(BF16)


def start_all(pairs, sems):
    copies = [pltpu.make_async_copy(src, dst, sems.at[i]) for i, (src, dst) in enumerate(pairs)]
    for copy in copies:
        copy.start()
    return copies


def payload_kernel(levels_ref, latents_ref, mods_ref, tok_ref, latents_here, mods_here, sems):
    tokens, width = latents_ref.shape
    level = levels_ref[0]
    group = pl.multiple_of(level // 8 * 8, 8)
    copies = start_all(
        [(mods_ref.at[:, pl.ds(group, 8), :], mods_here), (latents_ref, latents_here)], sems
    )
    copies[0].wait()
    chosen = lax.broadcasted_iota(jnp.int32, (8, width), 0) == level - group
    picked = [
        jnp.sum(jnp.where(chosen, mods_here[index], 0.0), axis=0, keepdims=True)
        for index in range(mods_here.shape[0])
    ]
    whole = jnp.concatenate(picked + picked[:2], axis=0)
    high = whole.astype(BF16).astype(F32)
    tok_ref[tokens:, :] = jnp.concatenate([high, whole - high], axis=0).astype(BF16)
    copies[1].wait()
    tok_ref[0:tokens, :] = latents_here[...]


def weight_kernel(
    map_ref, window_ref, qkv_ref, out_ref, packed_ref, window_here, qkv_here, out_here, sems
):
    lines, width = qkv_ref.shape
    rows = out_ref.shape[0]
    copies = start_all(
        [(window_ref, window_here), (qkv_ref, qkv_here), (out_ref, out_here)], sems
    )
    packed_ref[lines + 8 + rows :, :] = jnp.zeros((8, width), BF16)
    copies[0].wait()
    half = jnp.full((8, width), window_here[map_ref[0]].astype(F32))
    packed_ref[lines : lines + 8, :] = half.astype(BF16)
    copies[1].wait()
    packed_ref[0:lines, :] = qkv_here[...]
    copies[2].wait()
    packed_ref[lines + 8 : lines + 8 + rows, :] = out_here[...]


def join_mlp(fc1_ref, fc2_ref, to_ref, start, sems):
    hidden = fc2_ref.shape[0]
    return start_all(
        [
            (fc2_ref, to_ref.at[start : start + hidden]),
            (fc1_ref, to_ref.at[start + hidden : start + 2 * hidden]),
        ],
        sems,
    )


def whole_kernel(packed_ref, fc1_ref, fc2_ref, whole_ref, sems):
    start = packed_ref.shape[0]
    copies = join_mlp(fc1_ref, fc2_ref, whole_ref, start, sems)
    whole_ref[0:start, :] = packed_ref[...]
    for copy in copies:
        copy.wait()


def mod_of(tok_ref, tokens):
    terms = tok_ref[tokens:, :].astype(F32)
    return terms[0:8] + terms[8:16]


def fill(ref, value):
    rows = value.shape[0]
    for block in range(ref.shape[0] // rows):
        ref[block * rows : (block + 1) * rows, :] = value


def norm_kernel(tokens, tok_ref, normed_ref):
    mod = mod_of(tok_ref, tokens)
    fill(normed_ref, normalise(tok_ref[0:tokens, :].astype(F32), mod[0:1, :], mod[1:2, :]))


def project(head, normed, weight):
    return lax.dot_general(
        normed, weight[0 : 3 * head, :], (((1,), (1,)), ((), ())), preferred_element_type=F32
    )


def some_qkv_kernel(head, tok_ref, w0, w1, w2, fc1_ref, fc2_ref, part_ref, mlp_ref, sems):
    copies = join_mlp(fc1_ref, fc2_ref, mlp_ref, 0, sems)
    for slot, weight in enumerate((w0, w1, w2)):
        part_ref[slot, :, :] = project(head, tok_ref[...], weight).astype(BF16)
    for copy in copies:
        copy.wait()


def last_qkv_kernel(
    head, tok_ref, part_ref, w0, w1, w2, w3, q_ref, kv_ref, half_ref, outs_ref,
    q_here, half_here, outs_here, sems,
):
    first = 3 * head + 8
    weights = (w0, w1, w2, w3)
    outs = [ref[first : first + head, :].astype(F32) for ref in weights]
    outs_here[...] = jnp.concatenate(outs, axis=0).astype(BF16)
    copies = start_all([(outs_here, outs_ref)], sems)
    parts = [part_ref[slot].astype(F32) for slot in range(3)] + [project(head, tok_ref[...], w3)]
    query = jnp.concatenate([part[:, :head] for part in parts], axis=1)
    q_here[...] = query.astype(BF16)
    lane = lax.broadcasted_iota(jnp.int32, half_here.shape, 1)
    half = jnp.zeros(half_here.shape, F32)
    for slot, weight in enumerate(weights):
        mark = weight[3 * head - 8 : 3 * head + 8, 0:128].astype(F32)[8:16]
        half = jnp.where(lane == slot, mark, half)
    half_here[...] = half
    copies += start_all([(half_here, half_ref), (q_here, q_ref)], sems.at[1:3])
    keys = [part[:, head : 2 * head] for part in parts]
    keyval = jnp.concatenate(keys + [part[:, 2 * head :] for part in parts], axis=1)
    middle = keyval.shape[0] // 2
    kv_ref[...] = jnp.concatenate([keyval[:middle], keyval[middle:]], axis=1).astype(BF16)
    for copy in copies:
        copy.wait()


def indicators(head, cols):
    col = lax.broadcasted_iota(jnp.int32, (cols, 128), 0)
    lane = lax.broadcasted_iota(jnp.int32, (cols, 128), 1)
    gather = ((col >= lane * head) & (col < (lane + 1) * head)).astype(F32).astype(BF16)
    col = lax.broadcasted_iota(jnp.int32, (128, cols), 1)
    lane = lax.broadcasted_iota(jnp.int32, (128, cols), 0)
    spread = ((col >= lane * head) & (col < (lane + 1) * head)).astype(F32).astype(BF16)
    return gather, spread


def masked_scores(head, slots, place, half, query, gather, refs, offsets, reaches):
    rows, cols = query.shape
    frame = lax.rem(place + slots - 1, slots)
    products = [(query * unpack(ref, cols, 0)).astype(BF16) for ref in refs]
    scores = jnp.dot(jnp.concatenate(products, axis=0), gather, preferred_element_type=F32)
    masked, valids = [], []
    for index, (offset, reach) in enumerate(zip(offsets, reaches)):
        score = scores[index * rows : (index + 1) * rows] / (float(head) ** 0.5)
        target = frame + offset
        inside = ((target >= 0) & (target < slots)).astype(F32)
        valid = (inside * (half >= reach).astype(F32)) > 0.5
        valids.append(valid)
        masked.append(jnp.where(valid, score, -1e30))
    return masked, valids


def unpack(ref, cols, start):
    floats = ref[...].astype(F32)
    lanes = 2 * cols
    return jnp.concatenate(
        [floats[:, start : start + cols], floats[:, lanes + start : lanes + start + cols]], axis=0
    )


def early_kernel(
    head, slots, slot_ref, half_ref, q_ref, k0, k1, k2, outs_ref,
    half_here, q_here, outs_here, mixed_ref, top_ref, total_ref, sems,
):
    rows, cols = q_ref.shape
    copies = start_all([(half_ref, half_here), (q_ref, q_here), (outs_ref, outs_here)], sems)
    gather, spread = indicators(head, cols)
    place = slot_ref[0]
    copies[0].wait()
    copies[1].wait()
    refs = (k0, k1, k2)
    masked, valids = masked_scores(
        head, slots, place, half_here[0:1, :], q_here[...].astype(F32), gather, refs,
        (0, 2 * (place & 2) - 2, 2 * (place & 1) - 1), (0, 2, 1),
    )
    top = jnp.maximum(jnp.maximum(masked[0], masked[1]), masked[2])
    expo = [jnp.where(valid, jnp.exp(value - top), 0.0) for valid, value in zip(valids, masked)]
    top_ref[...] = top
    total_ref[...] = expo[0] + expo[1] + expo[2]
    wide = jnp.dot(
        jnp.concatenate(expo, axis=0).astype(BF16), spread, preferred_element_type=F32
    )
    mixed = jnp.zeros((rows, cols), F32)
    for index, ref in enumerate(refs):
        mixed = mixed + wide[index * rows : (index + 1) * rows] * unpack(ref, cols, cols)
    mixed_ref[...] = mixed
    copies[2].wait()


def late_kernel(
    head, slots, slot_ref, half_here, q_here, k3, k4, outs_here, mixed_ref, top_ref, total_ref, out_ref
):
    rows, cols = q_here.shape
    gather, spread = indicators(head, cols)
    place = slot_ref[0]
    refs = (k3, k4)
    masked, valids = masked_scores(
        head, slots, place, half_here[0:1, :], q_here[...].astype(F32), gather, refs,
        (2 - 2 * (place & 2), 1 - 2 * (place & 1)), (2, 1),
    )
    before = top_ref[...]
    top = jnp.maximum(jnp.maximum(masked[0], masked[1]), before)
    expo = [jnp.where(valid, jnp.exp(value - top), 0.0) for valid, value in zip(valids, masked)]
    scale = jnp.exp(before - top)
    total = total_ref[...] * scale + expo[0] + expo[1]
    shares = [(value / total).astype(BF16) for value in [scale] + expo]
    wide = jnp.dot(jnp.concatenate(shares, axis=0), spread, preferred_element_type=F32)
    mixed = wide[:rows] * mixed_ref[...]
    for index, ref in enumerate(refs):
        mixed = mixed + wide[(index + 1) * rows : (index + 2) * rows] * unpack(ref, cols, cols)
    out_ref[...] = jnp.dot(
        mixed.astype(BF16), outs_here[...], preferred_element_type=F32
    ).astype(BF16)


def total_of(parts_ref, tokens):
    total = parts_ref[0:tokens, :].astype(F32)
    for block in range(1, parts_ref.shape[0] // tokens):
        total = total + parts_ref[block * tokens : (block + 1) * tokens, :].astype(F32)
    return total


def resid_kernel(parts_ref, tok_ref, resid_ref, normed_ref):
    tokens = resid_ref.shape[0]
    mod = mod_of(tok_ref, tokens)
    attn = total_of(parts_ref, tokens)
    resid = (tok_ref[0:tokens, :].astype(F32) + mod[2:3, :] * attn).astype(BF16)
    resid_ref[...] = resid
    fill(normed_ref, normalise(resid.astype(F32), mod[3:4, :], mod[4:5, :]))


def mlp_of(hidden, normed, refs):
    first = jnp.concatenate([ref[ref.shape[0] - hidden :, :] for ref in refs], axis=0)
    wide = lax.dot_general(
        normed, first, (((1,), (1,)), ((), ())), preferred_element_type=F32
    )
    active = jax.nn.gelu(wide, approximate=True).astype(BF16)
    second = jnp.concatenate(
        [ref[ref.shape[0] - 2 * hidden : ref.shape[0] - hidden, :] for ref in refs], axis=0
    )
    return jnp.dot(active, second, preferred_element_type=F32)


def some_mlp_kernel(hidden, normed_ref, m0, m1, m2, sum_ref):
    sum_ref[...] = mlp_of(hidden, normed_ref[...], (m0, m1, m2))


def last_mlp_kernel(hidden, normed_ref, m3, sum_ref, part_ref):
    part_ref[...] = (sum_ref[...] + mlp_of(hidden, normed_ref[...], (m3,))).astype(BF16)


def final_kernel(slot_ref, parts_ref, resid_ref, tok_ref, fresh_ref, out_ref):
    tokens = resid_ref.shape[0]
    mod = mod_of(tok_ref, tokens)
    mlp = total_of(parts_ref, tokens)
    block_out = (resid_ref[...].astype(F32) + mod[5:6, :] * mlp).astype(BF16)
    out_ref[...] = jnp.where(slot_ref[0] == 0, fresh_ref[...].astype(F32), block_out.astype(F32)).astype(BF16)


SPECS = {
    "s": pl.BlockSpec(memory_space=pltpu.SMEM),
    "v": pl.BlockSpec(memory_space=pltpu.VMEM),
    "a": pl.BlockSpec(memory_space=pltpu.HBM),
}


def call(kernel, outs, kinds, *args, scratch=(), flops=0, limit=16):
    ins, back = ([SPECS[kind] for kind in part] for part in kinds.split(">"))
    args = [
        pltpu.with_memory_space_constraint(arg, pltpu.HBM) if kind == "a" else arg
        for arg, kind in zip(args, kinds)
    ]
    return pl.pallas_call(
        kernel,
        out_shape=outs,
        in_specs=ins,
        out_specs=tuple(back) if isinstance(outs, tuple) else back[0],
        scratch_shapes=scratch,
        compiler_params=pltpu.CompilerParams(vmem_limit_bytes=limit * MEGA),
        cost_estimate=pl.CostEstimate(flops=flops, bytes_accessed=1 << 20, transcendentals=0),
    )(*args)


def per_device(
    latents,
    fresh_noise,
    levels,
    modulation,
    head_map,
    window,
    qkv_weight,
    out_weight,
    fc1_weight,
    fc2_weight,
):
    tokens, width = latents.shape[1:]
    head = out_weight.shape[0]
    hidden = fc2_weight.shape[0]
    slots = lax.axis_size(SLOTS)
    slot = lax.axis_index(SLOTS)
    around = lax.axis_size("x")

    def shape(*dims, dtype=BF16):
        return jax.ShapeDtypeStruct(dims, dtype)

    payload = call(
        payload_kernel,
        shape(tokens + 16, width),
        "saa>v",
        levels,
        latents[0],
        modulation.transpose(1, 0, 2),
        scratch=[
            pltpu.VMEM((tokens, width), BF16),
            pltpu.VMEM((modulation.shape[1], 8, width), F32),
            pltpu.SemaphoreType.DMA((2,)),
        ],
    )
    moved = lax.ppermute(payload, SLOTS, [(s, (s + 1) % slots) for s in range(slots)])
    own_w = call(
        weight_kernel,
        shape(4 * head + 16, width),
        "saaa>v",
        head_map,
        window,
        qkv_weight.T,
        out_weight,
        scratch=[
            pltpu.SMEM(window.shape, jnp.int32),
            pltpu.VMEM((3 * head, width), BF16),
            pltpu.VMEM((head, width), BF16),
            pltpu.SemaphoreType.DMA((3,)),
        ],
    )
    near_w = lax.ppermute(own_w, "ylo", SWAP)
    far_w = lax.ppermute(own_w, ("yhi", "ylo", "core"), FAR)
    whole = call(
        whole_kernel,
        shape(4 * head + 16 + 2 * hidden, width),
        "vaa>v",
        own_w,
        fc1_weight.T,
        fc2_weight,
        scratch=[pltpu.SemaphoreType.DMA((2,))],
    )
    core_w = lax.ppermute(whole, "core", SWAP)
    rows = around * tokens
    cols = 4 * head
    normed = call(
        lambda *refs: norm_kernel(tokens, *refs), shape(rows, width), "v>v", moved, flops=100 * 10**9
    )
    tok = lax.all_to_all(normed, "x", 0, 0, tiled=True)
    part, own_m = call(
        lambda *refs: some_qkv_kernel(head, *refs),
        (shape(3, rows, 3 * head), shape(2 * hidden, width)),
        "vvvvaa>vv",
        tok,
        own_w,
        core_w,
        near_w,
        fc1_weight.T,
        fc2_weight,
        scratch=[pltpu.SemaphoreType.DMA((2,))],
    )
    query, keyval, halfs, outs = call(
        lambda *refs: last_qkv_kernel(head, *refs),
        (
            pltpu.HBM((rows, cols), BF16),
            shape(rows // 2, 4 * cols),
            pltpu.HBM((8, 128), F32),
            pltpu.HBM((cols, width), BF16),
        ),
        "vvvvvv>avaa",
        tok,
        part,
        own_w,
        core_w,
        near_w,
        far_w,
        scratch=[
            pltpu.VMEM((rows, cols), BF16),
            pltpu.VMEM((8, 128), F32),
            pltpu.VMEM((cols, width), BF16),
            pltpu.SemaphoreType.DMA((3,)),
        ],
    )
    ones = [(s, s ^ 1) for s in range(slots)]
    others = [(s, (((s - 1) ^ 1) + 1) % slots) for s in range(1, slots + 1)]
    others = [(s % slots, to) for s, to in others]
    twos = [(s, s ^ 2) for s in range(slots)]
    rest = [(s % slots, (((s - 2) ^ 2) + 2) % slots) for s in range(2, slots + 2)]
    arrived = [lax.ppermute(keyval, SLOTS, pairs) for pairs in (rest, others, twos, ones)]
    own_m, keyval = lax.optimization_barrier((own_m, keyval))
    near_m = lax.ppermute(own_m, "ylo", SWAP)
    far_m = lax.ppermute(own_m, ("yhi", "ylo", "core"), FAR)
    place = slot.astype(jnp.int32)[None]
    halfs, query, outs, mixed, top, total = call(
        lambda *refs: early_kernel(head, slots, *refs),
        (
            shape(8, 128, dtype=F32),
            shape(rows, cols),
            shape(cols, width),
            shape(rows, cols, dtype=F32),
            shape(rows, 128, dtype=F32),
            shape(rows, 128, dtype=F32),
        ),
        "saavvva>vvvvvv",
        place,
        halfs,
        query,
        keyval,
        *arrived[:2],
        outs,
        scratch=[pltpu.SemaphoreType.DMA((3,))],
    )
    attended = call(
        lambda *refs: late_kernel(head, slots, *refs),
        shape(rows, width),
        "svvvvvvvv>v",
        place,
        halfs,
        query,
        *arrived[2:],
        outs,
        mixed,
        top,
        total,
        flops=100 * 10**9,
    )
    parts = lax.all_to_all(attended, "x", 0, 0, tiled=True)
    resid, normed = call(
        resid_kernel, (shape(tokens, width), shape(rows, width)), "vv>vv", parts, moved
    )
    normed = lax.all_to_all(normed, "x", 0, 0, tiled=True)
    some = call(
        lambda *refs: some_mlp_kernel(hidden, *refs),
        shape(rows, width, dtype=F32),
        "vvvv>v",
        normed,
        own_m,
        core_w,
        near_m,
    )
    part = call(
        lambda *refs: last_mlp_kernel(hidden, *refs), shape(rows, width), "vvv>v", normed, far_m, some
    )
    parts = lax.all_to_all(part, "x", 0, 0, tiled=True)
    return call(
        final_kernel,
        shape(tokens, width),
        "svvvv>v",
        slot[None].astype(jnp.int32),
        parts,
        resid,
        moved,
        fresh_noise,
    )[None]


def solution(mesh):
    split = Mesh(mesh.devices.reshape(2, 16, 4, 2, 2), ("yhi", "z", "x", "ylo", "core"))
    mp = ("x", "ylo", "core")
    in_specs = (
        P(SLOTS, mp, None),
        P(mp, None),
        P(SLOTS),
        P(),
        P(mp),
        P(),
        P(None, mp),
        P(mp, None),
        P(None, mp),
        P(mp, None),
    )
    return jax.shard_map(
        per_device, mesh=split, in_specs=in_specs, out_specs=P(SLOTS, mp, None), check_vma=False
    )
```

```python
import jax
import jax.numpy as jnp
from jax import lax
from jax.experimental import pallas as pl
from jax.experimental.pallas import tpu as pltpu
from jax.sharding import Mesh
from jax.sharding import PartitionSpec as P

MEGA = 1024 * 1024
BF16, F32 = jnp.bfloat16, jnp.float32
SLOTS = ("yhi", "z")
SWAP = [(0, 1), (1, 0)]
FAR_Y = [(0, 3), (3, 0), (1, 2), (2, 1)]
FAR = [(2 * y + core, 2 * to + 1 - core) for y, to in FAR_Y for core in range(2)]


def normalise(floats, shift, scale):
    center = jnp.mean(floats, axis=-1, keepdims=True)
    spread = jnp.mean((floats - center) ** 2, axis=-1, keepdims=True)
    return ((floats - center) * lax.rsqrt(spread + 1e-06) * (1.0 + scale) + shift).astype(BF16)


def start_all(pairs, sems):
    copies = [pltpu.make_async_copy(src, dst, sems.at[i]) for i, (src, dst) in enumerate(pairs)]
    for copy in copies:
        copy.start()
    return copies


def payload_kernel(levels_ref, latents_ref, mods_ref, tok_ref, mods_here, sems):
    tokens, width = latents_ref.shape
    level = levels_ref[0]
    group = pl.multiple_of(level // 8 * 8, 8)
    copies = start_all(
        [(mods_ref.at[:, pl.ds(group, 8), :], mods_here), (latents_ref, tok_ref.at[0:tokens])], sems
    )
    copies[0].wait()
    chosen = lax.broadcasted_iota(jnp.int32, (8, width), 0) == level - group
    picked = [
        jnp.sum(jnp.where(chosen, mods_here[index], 0.0), axis=0, keepdims=True)
        for index in range(mods_here.shape[0])
    ]
    whole = jnp.concatenate(picked + picked[:2], axis=0)
    high = whole.astype(BF16).astype(F32)
    tok_ref[tokens:, :] = jnp.concatenate([high, whole - high], axis=0).astype(BF16)
    copies[1].wait()


def weight_kernel(
    map_ref, window_ref, qkv_ref, out_ref, packed_ref, window_here, qkv_here, out_here, sems
):
    width = qkv_ref.shape[1]
    rows = out_ref.shape[0]
    copies = start_all(
        [(window_ref, window_here), (qkv_ref, qkv_here), (out_ref, out_here)], sems
    )
    copies[0].wait()
    heads = lax.broadcasted_iota(jnp.int32, window_here.shape, 1)
    half = jnp.where(heads == map_ref[...], window_here[...].astype(F32), 0.0)
    half = jnp.broadcast_to(jnp.sum(half, axis=1, keepdims=True), (8, width))
    packed_ref[rows : rows + 8, :] = half.astype(BF16)
    copies[1].wait()
    packed_ref[rows + 8 :, :] = qkv_here[...]
    copies[2].wait()
    packed_ref[0:rows, :] = out_here[...]


def join_mlp(fc1_ref, fc2_ref, to_ref, start, sems):
    hidden = fc2_ref.shape[0]
    return start_all(
        [
            (fc2_ref, to_ref.at[start : start + hidden]),
            (fc1_ref, to_ref.at[start + hidden : start + 2 * hidden]),
        ],
        sems,
    )


def mod_of(tok_ref, tokens):
    terms = tok_ref[tokens:, :].astype(F32)
    return terms[0:8] + terms[8:16]


def fill(ref, value):
    rows = value.shape[0]
    for block in range(ref.shape[0] // rows):
        ref[block * rows : (block + 1) * rows, :] = value


def norm_kernel(tokens, tok_ref, normed_ref):
    mod = mod_of(tok_ref, tokens)
    fill(normed_ref, normalise(tok_ref[0:tokens, :].astype(F32), mod[0:1, :], mod[1:2, :]))


def project(head, normed, weight):
    return lax.dot_general(
        normed, weight[head + 8 :, :], (((1,), (1,)), ((), ())), preferred_element_type=F32
    )


def some_qkv_kernel(
    head, moved_ref, tok_ref, w0, w1, w2, fc1_ref, fc2_ref, part_ref, mlp_ref, kept_ref, outs_ref, sems
):
    count = head + 8
    weights = (w0, w1, w2)
    copies = join_mlp(fc1_ref, fc2_ref, mlp_ref, 0, sems)
    copies += start_all(
        [(ref.at[0:count], outs_ref.at[i]) for i, ref in enumerate(weights)]
        + [(moved_ref, kept_ref)],
        sems.at[2:6],
    )
    for slot, weight in enumerate(weights):
        part_ref[slot, :, :] = project(head, tok_ref[...], weight).astype(BF16)
    for copy in copies:
        copy.wait()


def last_qkv_kernel(
    head, tok_ref, part_ref, w0, w1, w2, w3, q_ref, kv_ref, half_ref, last_ref, q_here, half_here, sems
):
    weights = (w0, w1, w2, w3)
    copies = start_all([(w3.at[0 : head + 8], last_ref)], sems)
    parts = [part_ref[slot].astype(F32) for slot in range(3)] + [project(head, tok_ref[...], w3)]
    query = jnp.concatenate([part[:, :head] for part in parts], axis=1)
    q_here[...] = query.astype(BF16)
    copies += start_all([(q_here, q_ref)], sems.at[1:2])
    lane = lax.broadcasted_iota(jnp.int32, half_here.shape, 1)
    half = jnp.zeros(half_here.shape, F32)
    for slot, weight in enumerate(weights):
        mark = weight[head - 8 : head + 8, 0:128].astype(F32)[8:16]
        half = jnp.where(lane == slot, mark, half)
    half_here[...] = half
    copies += start_all([(half_here, half_ref)], sems.at[2:3])
    keys = [part[:, head : 2 * head] for part in parts]
    keyval = jnp.concatenate(keys + [part[:, 2 * head :] for part in parts], axis=1)
    middle = keyval.shape[0] // 2
    kv_ref[...] = jnp.concatenate([keyval[:middle], keyval[middle:]], axis=1).astype(BF16)
    for copy in copies:
        copy.wait()


def indicators(head, cols):
    col = lax.broadcasted_iota(jnp.int32, (cols, 128), 0)
    lane = lax.broadcasted_iota(jnp.int32, (cols, 128), 1)
    gather = ((col >= lane * head) & (col < (lane + 1) * head)).astype(F32).astype(BF16)
    col = lax.broadcasted_iota(jnp.int32, (128, cols), 1)
    lane = lax.broadcasted_iota(jnp.int32, (128, cols), 0)
    spread = ((col >= lane * head) & (col < (lane + 1) * head)).astype(F32).astype(BF16)
    return gather, spread


def masked_scores(head, slots, place, half, query, gather, keys, offsets, reaches):
    rows, cols = query.shape
    frame = lax.rem(place + slots - 1, slots)
    products = [(query * key).astype(BF16) for key in keys]
    scores = jnp.dot(jnp.concatenate(products, axis=0), gather, preferred_element_type=F32)
    masked, valids = [], []
    for index, (offset, reach) in enumerate(zip(offsets, reaches)):
        score = scores[index * rows : (index + 1) * rows] / (float(head) ** 0.5)
        target = frame + offset
        inside = ((target >= 0) & (target < slots)).astype(F32)
        valid = (inside * (half >= reach).astype(F32)) > 0.5
        valids.append(valid)
        masked.append(jnp.where(valid, score, -1e30))
    return masked, valids


def unpack(ref, cols, start):
    floats = ref[...].astype(F32)
    lanes = 2 * cols
    return jnp.concatenate(
        [floats[:, start : start + cols], floats[:, lanes + start : lanes + start + cols]], axis=0
    )


def early_kernel(
    head, slots, slot_ref, half_ref, q_ref, k0, k1, k2, outs_ref, last_ref,
    half_here, q_here, outs_here, mixed_ref, top_ref, total_ref, sems,
):
    rows, cols = q_ref.shape
    copies = start_all(
        [
            (half_ref, half_here),
            (q_ref, q_here),
            (outs_ref, outs_here.at[0:3]),
            (last_ref, outs_here.at[3]),
        ],
        sems,
    )
    gather, spread = indicators(head, cols)
    place = slot_ref[0]
    refs = (k0, k1, k2)
    keys = [unpack(ref, cols, 0) for ref in refs]
    copies[0].wait()
    copies[1].wait()
    masked, valids = masked_scores(
        head, slots, place, half_here[0:1, :], q_here[...].astype(F32), gather, keys,
        (0, 2 * (place & 2) - 2, 2 * (place & 1) - 1), (0, 2, 1),
    )
    top = jnp.maximum(jnp.maximum(masked[0], masked[1]), masked[2])
    expo = [jnp.where(valid, jnp.exp(value - top), 0.0) for valid, value in zip(valids, masked)]
    top_ref[...] = top
    total_ref[...] = expo[0] + expo[1] + expo[2]
    wide = jnp.dot(
        jnp.concatenate(expo, axis=0).astype(BF16), spread, preferred_element_type=F32
    )
    mixed = jnp.zeros((rows, cols), F32)
    for index, ref in enumerate(refs):
        mixed = mixed + wide[index * rows : (index + 1) * rows] * unpack(ref, cols, cols)
    mixed_ref[...] = mixed
    copies[2].wait()
    copies[3].wait()


def late_kernel(
    head, slots, slot_ref, half_here, q_here, k3, k4, outs_here, mixed_ref, top_ref, total_ref, out_ref
):
    rows, cols = q_here.shape
    gather, spread = indicators(head, cols)
    place = slot_ref[0]
    refs = (k3, k4)
    masked, valids = masked_scores(
        head, slots, place, half_here[0:1, :], q_here[...].astype(F32), gather,
        [unpack(ref, cols, 0) for ref in refs],
        (2 - 2 * (place & 2), 1 - 2 * (place & 1)), (2, 1),
    )
    before = top_ref[...]
    top = jnp.maximum(jnp.maximum(masked[0], masked[1]), before)
    expo = [jnp.where(valid, jnp.exp(value - top), 0.0) for valid, value in zip(valids, masked)]
    scale = jnp.exp(before - top)
    total = total_ref[...] * scale + expo[0] + expo[1]
    shares = [(value / total).astype(BF16) for value in [scale] + expo]
    wide = jnp.dot(jnp.concatenate(shares, axis=0), spread, preferred_element_type=F32)
    mixed = wide[:rows] * mixed_ref[...]
    for index, ref in enumerate(refs):
        mixed = mixed + wide[(index + 1) * rows : (index + 2) * rows] * unpack(ref, cols, cols)
    outs = [outs_here[slot].astype(F32)[0:head] for slot in range(4)]
    outs = jnp.concatenate(outs, axis=0).astype(BF16)
    out_ref[...] = jnp.dot(mixed.astype(BF16), outs, preferred_element_type=F32).astype(BF16)


def total_of(parts_ref, tokens):
    total = parts_ref[0:tokens, :].astype(F32)
    for block in range(1, parts_ref.shape[0] // tokens):
        total = total + parts_ref[block * tokens : (block + 1) * tokens, :].astype(F32)
    return total


def resid_kernel(parts_ref, tok_ref, resid_ref, normed_ref):
    tokens = resid_ref.shape[0]
    mod = mod_of(tok_ref, tokens)
    attn = total_of(parts_ref, tokens)
    resid = (tok_ref[0:tokens, :].astype(F32) + mod[2:3, :] * attn).astype(BF16)
    resid_ref[...] = resid
    fill(normed_ref, normalise(resid.astype(F32), mod[3:4, :], mod[4:5, :]))


def mlp_of(normed, ins, outs):
    wide = lax.dot_general(
        normed, jnp.concatenate(ins, axis=0), (((1,), (1,)), ((), ())), preferred_element_type=F32
    )
    active = jax.nn.gelu(wide, approximate=True).astype(BF16)
    return jnp.dot(active, jnp.concatenate(outs, axis=0), preferred_element_type=F32)


def some_mlp_kernel(hidden, normed_ref, m0, m1, m2, sum_ref):
    refs = (m0, m1, m2)
    ins, outs = [ref[hidden:, :] for ref in refs], [ref[0:hidden, :] for ref in refs]
    sum_ref[...] = mlp_of(normed_ref[...], ins, outs)


def last_mlp_kernel(hidden, normed_ref, m3, sum_ref, part_ref):
    last = mlp_of(normed_ref[...], [m3[hidden:, :]], [m3[0:hidden, :]])
    part_ref[...] = (sum_ref[...] + last).astype(BF16)


def final_kernel(slot_ref, parts_ref, resid_ref, tok_ref, fresh_ref, out_ref):
    tokens = resid_ref.shape[0]
    mod = mod_of(tok_ref, tokens)
    mlp = total_of(parts_ref, tokens)
    block_out = (resid_ref[...].astype(F32) + mod[5:6, :] * mlp).astype(BF16)
    out_ref[...] = jnp.where(slot_ref[0] == 0, fresh_ref[...].astype(F32), block_out.astype(F32)).astype(BF16)


SPECS = {
    "s": pl.BlockSpec(memory_space=pltpu.SMEM),
    "v": pl.BlockSpec(memory_space=pltpu.VMEM),
    "a": pl.BlockSpec(memory_space=pltpu.HBM),
}


def call(kernel, outs, kinds, *args, scratch=(), flops=0, limit=16):
    ins, back = ([SPECS[kind] for kind in part] for part in kinds.split(">"))
    args = [
        pltpu.with_memory_space_constraint(arg, pltpu.HBM) if kind == "a" else arg
        for arg, kind in zip(args, kinds)
    ]
    return pl.pallas_call(
        kernel,
        out_shape=outs,
        in_specs=ins,
        out_specs=tuple(back) if isinstance(outs, tuple) else back[0],
        scratch_shapes=scratch,
        compiler_params=pltpu.CompilerParams(vmem_limit_bytes=limit * MEGA),
        cost_estimate=pl.CostEstimate(flops=flops, bytes_accessed=1 << 20, transcendentals=0),
    )(*args)


def per_device(
    latents,
    fresh_noise,
    levels,
    modulation,
    head_map,
    window,
    qkv_weight,
    out_weight,
    fc1_weight,
    fc2_weight,
):
    tokens, width = latents.shape[1:]
    head = out_weight.shape[0]
    hidden = fc2_weight.shape[0]
    slots = lax.axis_size(SLOTS)
    slot = lax.axis_index(SLOTS)
    around = lax.axis_size("x")

    def shape(*dims, dtype=BF16):
        return jax.ShapeDtypeStruct(dims, dtype)

    payload = call(
        payload_kernel,
        shape(tokens + 16, width),
        "saa>v",
        levels,
        latents[0],
        modulation.transpose(1, 0, 2),
        scratch=[
            pltpu.VMEM((modulation.shape[1], 8, width), F32),
            pltpu.SemaphoreType.DMA((2,)),
        ],
    )
    moved = lax.ppermute(payload, SLOTS, [(s, (s + 1) % slots) for s in range(slots)])
    own_w = call(
        weight_kernel,
        shape(4 * head + 8, width),
        "vaaa>v",
        head_map.reshape(1, 1),
        window.reshape(1, -1),
        qkv_weight.T,
        out_weight,
        scratch=[
            pltpu.VMEM((1, window.shape[0]), jnp.int32),
            pltpu.VMEM((3 * head, width), BF16),
            pltpu.VMEM((head, width), BF16),
            pltpu.SemaphoreType.DMA((3,)),
        ],
    )
    core_w = lax.ppermute(lax.optimization_barrier((own_w, moved))[0], "core", SWAP)
    near_w = lax.ppermute(own_w, "ylo", SWAP)
    far_w = lax.ppermute(own_w, ("yhi", "ylo", "core"), FAR)
    rows = around * tokens
    cols = 4 * head
    normed = call(
        lambda *refs: norm_kernel(tokens, *refs), shape(rows, width), "v>v", moved, flops=100 * 10**9
    )
    tok = lax.all_to_all(normed, "x", 0, 0, tiled=True)
    part, own_m, kept, outs = call(
        lambda *refs: some_qkv_kernel(head, *refs),
        (
            shape(3, rows, 3 * head),
            shape(2 * hidden, width),
            pltpu.HBM(moved.shape, BF16),
            pltpu.HBM((3, head + 8, width), BF16),
        ),
        "vvvvvaa>vvaa",
        moved,
        tok,
        own_w,
        core_w,
        near_w,
        fc1_weight.T,
        fc2_weight,
        scratch=[pltpu.SemaphoreType.DMA((6,))],
    )
    query, keyval, halfs, last_out = call(
        lambda *refs: last_qkv_kernel(head, *refs),
        (
            pltpu.HBM((rows, cols), BF16),
            shape(rows // 2, 4 * cols),
            pltpu.HBM((8, 128), F32),
            pltpu.HBM((head + 8, width), BF16),
        ),
        "vvvvvv>avaa",
        tok,
        part,
        own_w,
        core_w,
        near_w,
        far_w,
        scratch=[
            pltpu.VMEM((rows, cols), BF16),
            pltpu.VMEM((8, 128), F32),
            pltpu.SemaphoreType.DMA((3,)),
        ],
    )
    ones = [(s, s ^ 1) for s in range(slots)]
    others = [(s, (((s - 1) ^ 1) + 1) % slots) for s in range(1, slots + 1)]
    others = [(s % slots, to) for s, to in others]
    twos = [(s, s ^ 2) for s in range(slots)]
    rest = [(s % slots, (((s - 2) ^ 2) + 2) % slots) for s in range(2, slots + 2)]
    arrived = [lax.ppermute(keyval, SLOTS, pairs) for pairs in (rest, others, twos, ones)]
    own_m, keyval = lax.optimization_barrier((own_m, keyval))
    near_m = lax.ppermute(own_m, "ylo", SWAP)
    far_m = lax.ppermute(own_m, ("yhi", "ylo", "core"), FAR)
    place = slot.astype(jnp.int32)[None]
    halfs, query, outs, mixed, top, total = call(
        lambda *refs: early_kernel(head, slots, *refs),
        (
            shape(8, 128, dtype=F32),
            shape(rows, cols),
            shape(4, head + 8, width),
            shape(rows, cols, dtype=F32),
            shape(rows, 128, dtype=F32),
            shape(rows, 128, dtype=F32),
        ),
        "saavvvaa>vvvvvv",
        place,
        halfs,
        query,
        keyval,
        *arrived[:2],
        outs,
        last_out,
        scratch=[pltpu.SemaphoreType.DMA((4,))],
    )
    core_m = lax.ppermute(lax.optimization_barrier((own_m, mixed))[0], "core", SWAP)
    attended = call(
        lambda *refs: late_kernel(head, slots, *refs),
        shape(rows, width),
        "svvvvvvvv>v",
        place,
        halfs,
        query,
        *arrived[2:],
        outs,
        mixed,
        top,
        total,
        flops=100 * 10**9,
    )
    parts = lax.all_to_all(attended, "x", 0, 0, tiled=True)
    resid, normed = call(
        resid_kernel, (shape(tokens, width), shape(rows, width)), "vv>vv", parts, kept
    )
    normed = lax.all_to_all(normed, "x", 0, 0, tiled=True)
    some = call(
        lambda *refs: some_mlp_kernel(hidden, *refs),
        shape(rows, width, dtype=F32),
        "vvvv>v",
        normed,
        own_m,
        core_m,
        near_m,
    )
    part = call(
        lambda *refs: last_mlp_kernel(hidden, *refs), shape(rows, width), "vvv>v", normed, far_m, some
    )
    parts = lax.all_to_all(part, "x", 0, 0, tiled=True)
    return call(
        final_kernel,
        shape(tokens, width),
        "svvvv>v",
        slot[None].astype(jnp.int32),
        parts,
        resid,
        kept,
        fresh_noise,
    )[None]


def solution(mesh):
    split = Mesh(mesh.devices.reshape(2, 16, 4, 2, 2), ("yhi", "z", "x", "ylo", "core"))
    mp = ("x", "ylo", "core")
    in_specs = (
        P(SLOTS, mp, None),
        P(mp, None),
        P(SLOTS),
        P(),
        P(mp),
        P(),
        P(None, mp),
        P(mp, None),
        P(None, mp),
        P(mp, None),
    )
    return jax.shard_map(
        per_device, mesh=split, in_specs=in_specs, out_specs=P(SLOTS, mp, None), check_vma=False
    )
```
